512 devices in a mesh: dp: 32 (over y, x_hi, core), tensor: 16 (over z, x_lo).
Axes of the slice: x: 4 (x_hi: 2, x_lo: 2; x = x_hi * 2 + x_lo), y: 8, z: 8, core: 2. Of those that a mesh axis runs over, the one named last changes fastest.
Arguments:
- ranks: int32 [28672], P('tensor'), may hold values from 0 to 28671, as said below
- down_weight: bfloat16 [28672, 8192], P('tensor', 'dp'), may hold values from -0.03125 to 0.03125
- inputs: bfloat16 [3, 256, 8192], P(None, 'tensor', 'dp'), may hold values from -6 to 6
- grad_out: bfloat16 [3, 256, 8192], P(None, 'tensor', 'dp'), may hold values from -0.29882812 to 0.29882812
- gate_small: bfloat16 [256, 7168], P('dp', 'tensor'), may hold values from -6 to 6
- up_small: bfloat16 [256, 7168], P('dp', 'tensor'), may hold values from -6 to 6
- gate_mid: bfloat16 [256, 14336], P('dp', 'tensor'), may hold values from -6 to 6
- up_mid: bfloat16 [256, 14336], P('dp', 'tensor'), may hold values from -6 to 6
- gate_full: bfloat16 [256, 28672], P('dp', 'tensor'), may hold values from -6 to 6
- up_full: bfloat16 [256, 28672], P('dp', 'tensor'), may hold values from -6 to 6
Outputs:
- down_grad: bfloat16 [28672, 8192], P('tensor', 'dp')
- gate_grad: bfloat16 [8192, 28672], P('dp', 'tensor')
- up_grad: bfloat16 [8192, 28672], P('dp', 'tensor')
The draws below stay inside these ranges and needn't reach their ends.
Inputs may be any that keep to these rules, and one draw needn't show every extreme that they name: ranks is a permutation of the neurons; the 28672 // 16 consecutive neurons of block j have exactly the ranks that leave remainder j when divided by 16.
All inputs are finite; a program needn't handle non-finite values.
Results may differ from the reference program's by a relative error of at most 0.0049.
Values may be sent and summed in bfloat16 or wider, within the bound.
No kernel may reach another device: no remote copies, remote signals or barrier semaphores. Data moves between devices by JAX's collectives and lax.ppermute only.
A program may use at most 64 MiB of HBM per device.

```python
import jax
import jax.numpy as jnp

D = 8192
FF = 28672
W_SMALL = 7168
W_MID = 14336
TOKENS = 256
N_TENSOR = 16


def draw_ranks(key, part):
    key = jax.random.fold_in(key, 7)
    shard_keys = jax.random.split(key, N_TENSOR)
    per_shard = FF // N_TENSOR
    shuffled = jax.vmap(lambda one_key: jax.random.permutation(one_key, per_shard))(shard_keys)
    shard_ids = jnp.arange(N_TENSOR, dtype=jnp.int32)[:, None]
    return (shard_ids + N_TENSOR * shuffled.astype(jnp.int32)).reshape(FF).astype(jnp.int32)


def level_of(stream_key, dims, pieces, least, largest):
    gain, own = 1.0, jax.random.fold_in(stream_key, 6)
    for dim, shards_of in pieces:
        heights = jnp.exp(jax.random.uniform(jax.random.fold_in(own, dim), (shards_of,), jnp.float32, least / len(pieces), largest / len(pieces)))
        gain = gain * jnp.repeat(heights, dims[dim] // shards_of).reshape([-1 if axis == dim else 1 for axis in range(len(dims))])
    return gain


def scatter_about(stream_key, shape, width, reach, shards=(), kind=jnp.bfloat16):
    result = jax.random.normal(stream_key, shape, jnp.float32) * width
    if len(shards) > 0:
        result = level_of(stream_key, shape, shards, -0.22, 0.18) * result
    return jnp.clip(result, min=-reach, max=reach).astype(kind)


def setup_inputs(seed: int = 0) -> dict:
    keys = jax.random.split(jax.random.key(seed), 11)
    return {
        "ranks": draw_ranks(jax.random.fold_in(keys[10], 71), 0),
        "down_weight": scatter_about(keys[1], (FF, D), FF ** -0.5, 0.03125, ((0, 16), (1, 32))),
        "inputs": scatter_about(keys[2], (3, TOKENS, D), 1.0, 6.0, ((1, 16), (2, 32))),
        "grad_out": scatter_about(keys[3], (3, TOKENS, D), 0.05, 0.29882812, ((1, 16), (2, 32))),
        "gate_small": scatter_about(keys[4], (TOKENS, W_SMALL), 1.0, 6.0, ((0, 32), (1, 16))),
        "up_small": scatter_about(keys[5], (TOKENS, W_SMALL), 1.0, 6.0, ((0, 32), (1, 16))),
        "gate_mid": scatter_about(keys[6], (TOKENS, W_MID), 1.0, 6.0, ((0, 32), (1, 16))),
        "up_mid": scatter_about(keys[7], (TOKENS, W_MID), 1.0, 6.0, ((0, 32), (1, 16))),
        "gate_full": scatter_about(keys[8], (TOKENS, FF), 1.0, 6.0, ((0, 32), (1, 16))),
        "up_full": scatter_about(keys[9], (TOKENS, FF), 1.0, 6.0, ((0, 32), (1, 16))),
    }


def rank_order(values, columns):
    count_rows = values.shape[0]
    return values.reshape(count_rows, N_TENSOR, columns // N_TENSOR).transpose(0, 2, 1).reshape(count_rows, columns)


def hidden_of(gate_value, up_value):
    gate_float = gate_value.astype(jnp.float32)
    up_float = up_value.astype(jnp.float32)
    return (gate_float * jax.nn.sigmoid(gate_float) * up_float).astype(jnp.bfloat16)


def slopes_of(gate_value, up_value, upstream):
    gate_float = gate_value.astype(jnp.float32)
    up_float = up_value.astype(jnp.float32)
    sigmoid_gate = jax.nn.sigmoid(gate_float)
    active = gate_float * sigmoid_gate
    gate_slope = (upstream * up_float * (sigmoid_gate * (1.0 + gate_float * (1.0 - sigmoid_gate)))).astype(jnp.bfloat16)
    up_slope = (upstream * active).astype(jnp.bfloat16)
    return gate_slope, up_slope


def nested_sum(lefts, rights):
    bounds = [0] + [item.shape[1] for item in lefts]
    blocks = []
    for index in range(3):
        start_col = bounds[index]
        stop_col = bounds[index + 1]
        total = jnp.zeros((stop_col - start_col, rights[0].shape[1]), jnp.float32)
        for source in range(index, 3):
            total = total + jnp.dot(lefts[source][:, start_col:stop_col].T, rights[source], preferred_element_type=jnp.float32)
        blocks.append(total.astype(jnp.bfloat16))
    return jnp.concatenate(blocks, 0)


def reference(ranks, down_weight, inputs, grad_out, gate_small, up_small, gate_mid, up_mid, gate_full, up_full):
    by_rank = jnp.argsort(ranks).astype(jnp.int32)
    ranked_down = jnp.take(down_weight, by_rank, axis=0)
    pairs = ((gate_small, up_small), (gate_mid, up_mid), (gate_full, up_full))
    hiddens = []
    gate_slopes = []
    up_slopes = []
    for index in range(3):
        gate_value, up_value = pairs[index]
        columns = gate_value.shape[1]
        gate_ranked = rank_order(gate_value, columns)
        up_ranked = rank_order(up_value, columns)
        upstream = jnp.dot(grad_out[index], ranked_down[:columns].T, preferred_element_type=jnp.float32)
        hiddens.append(hidden_of(gate_ranked, up_ranked))
        gate_slope, up_slope = slopes_of(gate_ranked, up_ranked, upstream)
        gate_slopes.append(gate_slope)
        up_slopes.append(up_slope)
    grad_list = [grad_out[index] for index in range(3)]
    input_list = [inputs[index] for index in range(3)]
    down_ranked = nested_sum(hiddens, grad_list)
    down_grad = jnp.take(down_ranked, ranks, axis=0)
    gate_ranked_grad = nested_sum(gate_slopes, input_list)
    gate_grad = jnp.take(gate_ranked_grad, ranks, axis=0).T
    up_ranked_grad = nested_sum(up_slopes, input_list)
    up_grad = jnp.take(up_ranked_grad, ranks, axis=0).T
    return down_grad, gate_grad, up_grad
```

```python
import functools

import jax
import jax.numpy as jnp
from jax import lax
from jax.experimental import pallas as pl
from jax.experimental.pallas import tpu as pltpu
from jax.sharding import PartitionSpec as P

VMEM = pl.BlockSpec(memory_space=pltpu.VMEM)
SMEM = pl.BlockSpec(memory_space=pltpu.SMEM)
LIMIT = pltpu.CompilerParams(vmem_limit_bytes=48 * 1024 * 1024)
TILE = 256


def padded(width):
    return -(-width // 128) * 128


def sort_kernel(position, down, ranked):
    count = down.shape[0]

    @pl.loop(0, count // TILE)
    def _(block):
        start = pl.multiple_of(block * TILE, TILE)
        rows = lax.broadcasted_iota(jnp.int32, (TILE, count), 0) + start
        chosen = (rows == position[...]).astype(jnp.float32).astype(jnp.bfloat16)
        ranked[pl.ds(start, TILE), :] = jnp.dot(
            chosen, down[...], preferred_element_type=jnp.float32
        ).astype(jnp.bfloat16)


def partial_kernel(widths, half, tokens, ranked, out):
    blocks = tokens.shape[0] // 2
    rows = blocks * tokens.shape[2]
    first = half[0] * blocks
    offset = 0
    for index, width in enumerate(widths):
        left = tokens[pl.ds(first, blocks), index].reshape(rows, tokens.shape[3])
        out[:, offset : offset + width] = lax.dot_general(
            left, ranked[:width], (((1,), (1,)), ((), ())), preferred_element_type=jnp.float32
        ).astype(out.dtype)
        offset += width


def final_kernel(
    widths, position, gate_up, upstream, tokens, down_grad, gate_grad, up_grad, hidden, gates, ups, totals
):
    count = position.shape[1]
    rows = gate_up.shape[0]
    features = tokens.shape[3]
    offset = 0
    for width in widths:
        step = 128

        @pl.loop(0, width // step)
        def _(block, offset=offset, width=width):
            start = pl.multiple_of(block * step, step)
            gate = gate_up[:, pl.ds(2 * offset + start, step)].astype(jnp.float32)
            up = gate_up[:, pl.ds(2 * offset + width + start, step)].astype(jnp.float32)
            place = pl.ds(offset + start, step)
            above = upstream[:, place].astype(jnp.float32)
            sigmoid = jax.nn.sigmoid(gate)
            active = gate * sigmoid
            hidden[:, place] = (active * up).astype(jnp.bfloat16)
            gates[:, place] = (above * up * (sigmoid * (1.0 + gate * (1.0 - sigmoid)))).astype(
                jnp.bfloat16
            )
            ups[:, place] = (above * active).astype(jnp.bfloat16)

        offset += width

    starts = (0, widths[0], widths[0] + widths[1])
    bounds = (0,) + widths
    sources = ((hidden, 3), (gates, 0), (ups, 0))
    for which, (array, base) in enumerate(sources):
        for band in range(3):
            low, high = bounds[band], bounds[band + 1]
            total = None
            for index in range(band, 3):
                left = tokens[:, base + index].reshape(rows, features)
                term = lax.dot_general(
                    left,
                    array[:, starts[index] + low : starts[index] + high],
                    (((0,), (0,)), ((), ())),
                    preferred_element_type=jnp.float32,
                )
                total = term if total is None else total + term
            totals[which * features : (which + 1) * features, low:high] = total.astype(jnp.bfloat16)

    @pl.loop(0, count // TILE)
    def _(block):
        start = pl.multiple_of(block * TILE, TILE)
        ranks_here = lax.broadcasted_iota(jnp.int32, (count, TILE), 0)
        chosen = (ranks_here == position[:, pl.ds(start, TILE)]).astype(jnp.float32).astype(jnp.bfloat16)
        moved = jnp.dot(totals[...], chosen, preferred_element_type=jnp.float32)
        down_grad[pl.ds(start, TILE), :] = moved[:features].T.astype(jnp.bfloat16)
        gate_grad[:, pl.ds(start, TILE)] = moved[features : 2 * features].astype(jnp.bfloat16)
        up_grad[:, pl.ds(start, TILE)] = moved[2 * features :].astype(jnp.bfloat16)


def sort_rows(position, down):
    return pl.pallas_call(
        sort_kernel,
        out_shape=jax.ShapeDtypeStruct(down.shape, jnp.bfloat16),
        in_specs=[VMEM, VMEM],
        out_specs=VMEM,
        compiler_params=LIMIT,
    )(position, down)


def partial_of(widths, half, tokens, ranked, dtype):
    rows = tokens.shape[0] // 2 * tokens.shape[2]
    return pl.pallas_call(
        functools.partial(partial_kernel, widths),
        out_shape=jax.ShapeDtypeStruct((rows, sum(widths)), dtype),
        in_specs=[SMEM, VMEM, VMEM],
        out_specs=VMEM,
        compiler_params=LIMIT,
    )(half, tokens, ranked)


def finish(widths, position, gate_up, upstream, tokens):
    count = position.shape[1]
    rows = gate_up.shape[0]
    features = tokens.shape[3]
    return pl.pallas_call(
        functools.partial(final_kernel, widths),
        out_shape=(
            jax.ShapeDtypeStruct((count, features), jnp.bfloat16),
            jax.ShapeDtypeStruct((features, count), jnp.bfloat16),
            jax.ShapeDtypeStruct((features, count), jnp.bfloat16),
        ),
        in_specs=[VMEM] * 4,
        out_specs=(VMEM,) * 3,
        scratch_shapes=[pltpu.VMEM((rows, sum(widths)), jnp.bfloat16)] * 3
        + [pltpu.VMEM((3 * features, count), jnp.bfloat16)],
        compiler_params=LIMIT,
    )(position, gate_up, upstream, tokens)


def per_device(
    ranks, down_weight, inputs, grad_out, gate_small, up_small, gate_mid, up_mid, gate_full, up_full
):
    n_dp = lax.axis_size("dp")
    n_tensor = lax.axis_size("tensor")
    chips = n_dp // 2
    widths = tuple(padded(item.shape[1]) for item in (gate_small, gate_mid, gate_full))
    total = sum(widths)

    pairs = ((gate_small, up_small), (gate_mid, up_mid), (gate_full, up_full))
    local = jnp.concatenate(
        [
            jnp.pad(item, ((0, 0), (0, width - item.shape[1])))
            for pair, width in zip(pairs, widths)
            for item in pair
        ],
        axis=1,
    )
    gate_up = lax.all_gather(local, "dp", axis=0, tiled=True)

    position = (ranks // n_tensor)[None, :]
    ranked = sort_rows(position, down_weight)

    own = jnp.concatenate([inputs, grad_out], axis=0)
    tokens = lax.all_to_all(
        jnp.broadcast_to(own[None], (n_tensor,) + own.shape), "tensor", 0, 0, tiled=True
    )

    core = lax.axis_index("dp") % 2
    grads = tokens[:, 3:]
    sent = partial_of(widths, (1 - core)[None], grads, ranked, jnp.bfloat16)
    other = lax.ppermute(sent, "dp", [(item, item ^ 1) for item in range(n_dp)])
    kept = partial_of(widths, core[None], grads, ranked, jnp.float32)
    summed = (kept + other.astype(jnp.float32)).astype(jnp.bfloat16)

    by_core = [[2 * chip + side for chip in range(chips)] for side in range(2)]
    block = summed.shape[0] // chips
    pieces = lax.all_to_all(
        summed.reshape(chips, block, total), "dp", 0, 0, axis_index_groups=by_core, tiled=True
    )
    reduced = jnp.sum(pieces.astype(jnp.float32), axis=0).astype(jnp.bfloat16)
    spread = lax.all_to_all(
        jnp.broadcast_to(reduced[None], (chips, block, total)),
        "dp",
        0,
        0,
        axis_index_groups=by_core,
        tiled=True,
    ).reshape(chips * block, total)
    by_chip = [[2 * chip, 2 * chip + 1] for chip in range(chips)]
    upstream = lax.all_gather(spread, "dp", axis=0, axis_index_groups=by_chip, tiled=True)
    return finish(widths, position, gate_up, upstream, tokens)


def solution(mesh):
    return jax.shard_map(
        per_device,
        mesh=mesh,
        in_specs=(
            P("tensor"),
            P("tensor", "dp"),
            P(None, "tensor", "dp"),
            P(None, "tensor", "dp"),
            P("dp", "tensor"),
            P("dp", "tensor"),
            P("dp", "tensor"),
            P("dp", "tensor"),
            P("dp", "tensor"),
            P("dp", "tensor"),
        ),
        out_specs=(P("tensor", "dp"), P("dp", "tensor"), P("dp", "tensor")),
        check_vma=False,
    )
```

```python
import functools

import jax
import jax.numpy as jnp
from jax import lax
from jax.experimental import pallas as pl
from jax.experimental.pallas import tpu as pltpu
from jax.sharding import PartitionSpec as P

VMEM = pl.BlockSpec(memory_space=pltpu.VMEM)
SMEM = pl.BlockSpec(memory_space=pltpu.SMEM)
LIMIT = pltpu.CompilerParams(vmem_limit_bytes=48 * 1024 * 1024)
TILE = 256


def padded(width):
    return -(-width // 128) * 128


def sort_kernel(position, down, ranked):
    count = down.shape[0]

    @pl.loop(0, count // TILE)
    def _(block):
        start = pl.multiple_of(block * TILE, TILE)
        rows = lax.broadcasted_iota(jnp.int32, (TILE, count), 0) + start
        chosen = (rows == position[...]).astype(jnp.float32).astype(jnp.bfloat16)
        ranked[pl.ds(start, TILE), :] = jnp.dot(
            chosen, down[...], preferred_element_type=jnp.float32
        ).astype(jnp.bfloat16)


def split_sides(block, side):
    rows = block.shape[1] // 2
    pair = block.astype(jnp.float32).reshape(block.shape[0], 2, rows, block.shape[2])
    own = jnp.where(side == 0, pair[:, 0], pair[:, 1])
    other = jnp.where(side == 0, pair[:, 1], pair[:, 0])
    flat = (block.shape[0] * rows, block.shape[2])
    return own.reshape(flat).astype(jnp.bfloat16), other.reshape(flat).astype(jnp.bfloat16)


def partial_kernel(widths, side, tokens, ranked, out):
    offset = 0
    for index, width in enumerate(widths):
        left, _ = split_sides(tokens[:, 3 + index], side[0])
        out[:, offset : offset + width] = lax.dot_general(
            left, ranked[:width], (((1,), (1,)), ((), ())), preferred_element_type=jnp.float32
        ).astype(out.dtype)
        offset += width


def banded(widths, sides, array, stored, low_row):
    bounds = (0,) + widths
    starts = (0, widths[0], widths[0] + widths[1])
    features = sides[0].shape[1]
    for band in range(3):
        low, high = bounds[band], bounds[band + 1]
        total = None
        for index in range(band, 3):
            term = lax.dot_general(
                sides[index],
                array[:, starts[index] + low : starts[index] + high],
                (((0,), (0,)), ((), ())),
                preferred_element_type=jnp.float32,
            )
            total = term if total is None else total + term
        stored[low_row : low_row + features, low:high] = total.astype(jnp.bfloat16)


def chosen_ranks(position, start):
    count = position.shape[1]
    ranks_here = lax.broadcasted_iota(jnp.int32, (count, TILE), 0)
    return (ranks_here == position[:, pl.ds(start, TILE)]).astype(jnp.float32).astype(jnp.bfloat16)


def hidden_kernel(
    widths, side, position, pairs, tokens, down_grad, gate_rate, up_rate, hidden, totals
):
    count = position.shape[1]
    features = tokens.shape[3]
    rows = pairs.shape[0] * pairs.shape[2]
    offset = 0
    for width in widths:
        step = 128

        @pl.loop(0, width // step)
        def _(block, offset=offset, width=width):
            start = pl.multiple_of(block * step, step)
            place = pl.ds(offset + start, step)
            for row, which in ((0, side[0]), (rows, 1 - side[0])):
                gate = pairs[:, which, :, pl.ds(2 * offset + start, step)].astype(jnp.float32)
                up = pairs[:, which, :, pl.ds(2 * offset + width + start, step)].astype(jnp.float32)
                gate = gate.reshape(rows, step)
                up = up.reshape(rows, step)
                sigmoid = jax.nn.sigmoid(gate)
                active = gate * sigmoid
                hidden[row : row + rows, place] = (active * up).astype(jnp.bfloat16)
                gate_rate[row : row + rows, place] = up * (sigmoid * (1.0 + gate * (1.0 - sigmoid)))
                up_rate[row : row + rows, place] = active

        offset += width

    sides = [
        jnp.concatenate(split_sides(tokens[:, 3 + index], side[0]), axis=0) for index in range(3)
    ]
    banded(widths, sides, hidden, totals, 0)

    @pl.loop(0, count // TILE)
    def _(block):
        start = pl.multiple_of(block * TILE, TILE)
        moved = jnp.dot(
            totals[...], chosen_ranks(position, start), preferred_element_type=jnp.float32
        )
        down_grad[pl.ds(start, TILE), :] = moved.T.astype(jnp.bfloat16)


def slopes_kernel(
    widths, side, position, own_up, other_up, gate_rate, up_rate, tokens, gate_grad, up_grad, gates, ups, totals
):
    count = position.shape[1]
    features = tokens.shape[3]
    rows = own_up.shape[0]
    step = 128

    @pl.loop(0, sum(widths) // step)
    def _(block):
        place = pl.ds(pl.multiple_of(block * step, step), step)
        for row, above in ((0, own_up), (rows, other_up)):
            upstream = above[:, place].astype(jnp.float32)
            gates[row : row + rows, place] = (
                upstream * gate_rate[row : row + rows, place]
            ).astype(jnp.bfloat16)
            ups[row : row + rows, place] = (
                upstream * up_rate[row : row + rows, place]
            ).astype(jnp.bfloat16)

    sides = [jnp.concatenate(split_sides(tokens[:, index], side[0]), axis=0) for index in range(3)]
    banded(widths, sides, gates, totals, 0)
    banded(widths, sides, ups, totals, features)

    @pl.loop(0, count // TILE)
    def _(block):
        start = pl.multiple_of(block * TILE, TILE)
        moved = jnp.dot(
            totals[...], chosen_ranks(position, start), preferred_element_type=jnp.float32
        )
        gate_grad[:, pl.ds(start, TILE)] = moved[:features].astype(jnp.bfloat16)
        up_grad[:, pl.ds(start, TILE)] = moved[features:].astype(jnp.bfloat16)


def sort_rows(position, down):
    return pl.pallas_call(
        sort_kernel,
        out_shape=jax.ShapeDtypeStruct(down.shape, jnp.bfloat16),
        in_specs=[VMEM, VMEM],
        out_specs=VMEM,
        compiler_params=LIMIT,
    )(position, down)


def partial_of(widths, side, tokens, ranked, dtype):
    rows = tokens.shape[0] * tokens.shape[2] // 2
    return pl.pallas_call(
        functools.partial(partial_kernel, widths),
        out_shape=jax.ShapeDtypeStruct((rows, sum(widths)), dtype),
        in_specs=[SMEM, VMEM, VMEM],
        out_specs=VMEM,
        compiler_params=LIMIT,
        cost_estimate=pl.CostEstimate(
            flops=2 * rows * sum(widths) * tokens.shape[3],
            bytes_accessed=2 * 2**20,
            transcendentals=0,
        ),
    )(side, tokens, ranked)


def after(value, other):
    def nothing(value_ref, other_ref, out_ref):
        pass

    return pl.pallas_call(
        nothing,
        out_shape=jax.ShapeDtypeStruct(value.shape, value.dtype),
        in_specs=[pl.BlockSpec(memory_space=pl.ANY)] * 2,
        out_specs=pl.BlockSpec(memory_space=pl.ANY),
        input_output_aliases={0: 0},
    )(value, other)


def hidden_parts(widths, side, position, pairs, tokens):
    count = position.shape[1]
    rows = 2 * pairs.shape[0] * pairs.shape[2]
    features = tokens.shape[3]
    columns = sum(widths)
    return pl.pallas_call(
        functools.partial(hidden_kernel, widths),
        out_shape=(
            jax.ShapeDtypeStruct((count, features), jnp.bfloat16),
            jax.ShapeDtypeStruct((rows, columns), jnp.float32),
            jax.ShapeDtypeStruct((rows, columns), jnp.float32),
        ),
        in_specs=[SMEM] + [VMEM] * 3,
        out_specs=(VMEM,) * 3,
        scratch_shapes=[
            pltpu.VMEM((rows, columns), jnp.bfloat16),
            pltpu.VMEM((features, count), jnp.bfloat16),
        ],
        compiler_params=LIMIT,
        cost_estimate=pl.CostEstimate(
            flops=2 * features * count * (count + rows), bytes_accessed=8 * 2**20, transcendentals=0
        ),
    )(side, position, pairs, tokens)


def slopes_parts(widths, side, position, own_up, other_up, gate_rate, up_rate, tokens):
    count = position.shape[1]
    rows = 2 * own_up.shape[0]
    features = tokens.shape[3]
    columns = sum(widths)
    return pl.pallas_call(
        functools.partial(slopes_kernel, widths),
        out_shape=(jax.ShapeDtypeStruct((features, count), jnp.bfloat16),) * 2,
        in_specs=[SMEM] + [VMEM] * 6,
        out_specs=(VMEM,) * 2,
        scratch_shapes=[pltpu.VMEM((rows, columns), jnp.bfloat16)] * 2
        + [pltpu.VMEM((2 * features, count), jnp.bfloat16)],
        compiler_params=LIMIT,
        cost_estimate=pl.CostEstimate(
            flops=4 * features * count * (count + rows), bytes_accessed=8 * 2**20, transcendentals=0
        ),
    )(side, position, own_up, other_up, gate_rate, up_rate, tokens)


def per_device(
    ranks, down_weight, inputs, grad_out, gate_small, up_small, gate_mid, up_mid, gate_full, up_full
):
    n_dp = lax.axis_size("dp")
    n_tensor = lax.axis_size("tensor")
    chips = n_dp // 2
    side = (lax.axis_index("dp") % 2)[None]
    swap = [(item, item ^ 1) for item in range(n_dp)]
    by_core = [[2 * chip + side for chip in range(chips)] for side in range(2)]
    widths = tuple(padded(item.shape[1]) for item in (gate_small, gate_mid, gate_full))
    total = sum(widths)

    def copies_to_chips(piece):
        return lax.all_to_all(
            jnp.broadcast_to(piece[None], (chips,) + piece.shape),
            "dp",
            0,
            0,
            axis_index_groups=by_core,
            tiled=True,
        ).reshape(-1, piece.shape[1])

    own = jnp.concatenate([inputs, grad_out], axis=0)
    tokens = lax.all_to_all(
        jnp.broadcast_to(own[None], (n_tensor,) + own.shape), "tensor", 0, 0, tiled=True
    )

    given = ((gate_small, up_small), (gate_mid, up_mid), (gate_full, up_full))
    local = jnp.concatenate(
        [
            jnp.pad(item, ((0, 0), (0, width - item.shape[1])))
            for pair, width in zip(given, widths)
            for item in pair
        ],
        axis=1,
    )
    across = [(item, item ^ 2) for item in range(n_dp)]
    there = lax.ppermute(local, "dp", across)
    first = (lax.axis_index("dp") // 2) % 2 == 0
    two = jnp.concatenate([jnp.where(first, local, there), jnp.where(first, there, local)], axis=0)
    by_side = [
        [4 * row + 2 * half + core for row in range(n_dp // 4) for core in range(2)] for half in range(2)
    ]
    gathered = lax.all_gather(two, "dp", axis=0, axis_index_groups=by_side, tiled=True)
    pairs = gathered.reshape(n_dp // 4, 2, two.shape[0], two.shape[1])

    position = (ranks // n_tensor)[None, :]
    ranked = sort_rows(position, down_weight)

    sent = partial_of(widths, 1 - side, tokens, ranked, jnp.bfloat16)
    other = lax.ppermute(sent, "dp", swap)
    kept = partial_of(widths, side, tokens, ranked, jnp.float32)
    summed = (kept + other.astype(jnp.float32)).astype(jnp.bfloat16)

    pieces = lax.all_to_all(
        summed.reshape(chips, -1, total), "dp", 0, 0, axis_index_groups=by_core, tiled=True
    )
    reduced = jnp.sum(pieces.astype(jnp.float32), axis=0).astype(jnp.bfloat16)
    own_up = copies_to_chips(reduced)
    down_grad, gate_rate, up_rate = hidden_parts(
        widths, side, position, pairs, tokens
    )
    own_up = after(own_up, gate_rate)
    other_up = lax.ppermute(own_up, "dp", swap)

    gate_grad, up_grad = slopes_parts(
        widths, side, position, own_up, other_up, gate_rate, up_rate, tokens
    )
    return (down_grad, gate_grad, up_grad)


def solution(mesh):
    return jax.shard_map(
        per_device,
        mesh=mesh,
        in_specs=(
            P("tensor"),
            P("tensor", "dp"),
            P(None, "tensor", "dp"),
            P(None, "tensor", "dp"),
            P("dp", "tensor"),
            P("dp", "tensor"),
            P("dp", "tensor"),
            P("dp", "tensor"),
            P("dp", "tensor"),
            P("dp", "tensor"),
        ),
        out_specs=(P("tensor", "dp"), P("dp", "tensor"), P("dp", "tensor")),
        check_vma=False,
    )
```

```python
import functools

import jax
import jax.numpy as jnp
from jax import lax
from jax.experimental import pallas as pl
from jax.experimental.pallas import tpu as pltpu
from jax.sharding import PartitionSpec as P

VMEM = pl.BlockSpec(memory_space=pltpu.VMEM)
ANY = pl.BlockSpec(memory_space=pl.ANY)
SMEM = pl.BlockSpec(memory_space=pltpu.SMEM)
LIMIT = pltpu.CompilerParams(vmem_limit_bytes=20 * 1024 * 1024)
FULL = pltpu.CompilerParams(vmem_limit_bytes=50 * 1024 * 1024)
TILE = 256
STEP = 128


def padded(width):
    return -(-width // 128) * 128


def call(kernel, out_shape, *args, scratch=(), scalars=0, flops=0):
    many = isinstance(out_shape, tuple)
    return pl.pallas_call(
        kernel,
        out_shape=out_shape,
        in_specs=[SMEM] * scalars + [VMEM] * (len(args) - scalars),
        out_specs=(VMEM,) * len(out_shape) if many else VMEM,
        scratch_shapes=list(scratch),
        compiler_params=LIMIT,
        cost_estimate=pl.CostEstimate(flops=flops, bytes_accessed=2**20, transcendentals=0),
    )(*args)


def shaped(shape, dtype=jnp.bfloat16):
    return jax.ShapeDtypeStruct(shape, dtype)


def after(value, other):
    def nothing(value_ref, other_ref, out_ref):
        pass

    return pl.pallas_call(
        nothing,
        out_shape=shaped(value.shape, value.dtype),
        in_specs=[VMEM, VMEM],
        out_specs=VMEM,
        input_output_aliases={0: 0},
        compiler_params=LIMIT,
    )(value, other)


def start_kernel(*refs):
    far, copies, packed = refs[:8], refs[8], refs[9]
    near, sems = refs[10:18], refs[18]
    moves = [
        pltpu.make_async_copy(source, target, sems.at[index])
        for index, (source, target) in enumerate(zip(far, near))
    ]
    for move in moves:
        move.start()
    for move in moves[:6]:
        move.wait()
    offset = 0
    for array in near[:6]:
        width = array.shape[1]
        wide = padded(width)
        if wide != width:
            packed[:, offset : offset + wide] = jnp.zeros((packed.shape[0], wide), packed.dtype)
        packed[:, offset : offset + width] = array[...]
        offset += wide
    for move in moves[6:]:
        move.wait()
    count = near[6].shape[0]

    @pl.loop(0, copies.shape[0])
    def _(place):
        copies[place, :count] = near[6][...]
        copies[place, count:] = near[7][...]


def sort_kernel(position, down, ranked, chosen):
    count = down.shape[0]

    @pl.loop(0, count // TILE)
    def _(block):
        here = pl.ds(pl.multiple_of(block * TILE, TILE), TILE)
        rows = lax.broadcasted_iota(jnp.int32, (TILE, count), 0) + block * TILE
        ones = (rows == position[...]).astype(jnp.float32).astype(jnp.bfloat16)
        chosen[here, :] = ones
        ranked[here, :] = jnp.dot(ones, down[...], preferred_element_type=jnp.float32).astype(
            jnp.bfloat16
        )


def split_sides(block, side):
    rows = block.shape[1] // 2
    pair = block.astype(jnp.float32).reshape(block.shape[0], 2, rows, block.shape[2])
    own = jnp.where(side == 0, pair[:, 0], pair[:, 1])
    other = jnp.where(side == 0, pair[:, 1], pair[:, 0])
    flat = (block.shape[0] * rows, block.shape[2])
    return own.reshape(flat), other.reshape(flat)


def partial_kernel(widths, side, tokens, ranked, out):
    offset = 0
    for index, width in enumerate(widths):
        left, _ = split_sides(tokens[:, 3 + index], side[0])
        out[:, offset : offset + width] = lax.dot_general(
            left.astype(jnp.bfloat16),
            ranked[:width],
            (((1,), (1,)), ((), ())),
            preferred_element_type=jnp.float32,
        ).astype(out.dtype)
        offset += width


def banded(widths, across, stacked, stored, low_row):
    bounds = (0,) + widths
    features, tokens = across.shape[0], across.shape[1] // 3
    for band in range(3):
        low, high = bounds[band], bounds[band + 1]
        stored[low_row : low_row + features, low:high] = jnp.dot(
            across[:, band * tokens :],
            stacked[band * tokens :, low:high],
            preferred_element_type=jnp.float32,
        ).astype(jnp.bfloat16)


def hidden_kernel(
    widths, side, chosen, pairs, tokens, down_grad, rates, turned, hidden, totals, turned_out
):
    count = chosen.shape[0]
    rows = pairs.shape[0] * pairs.shape[2]
    offset = 0
    for index, width in enumerate(widths):

        @pl.loop(0, width // STEP)
        def _(block, index=index, offset=offset, width=width):
            start = pl.multiple_of(block * STEP, STEP)
            for half, which in ((0, side[0]), (1, 1 - side[0])):
                gate = pairs[:, which, :, pl.ds(2 * offset + start, STEP)].astype(jnp.float32)
                up = pairs[:, which, :, pl.ds(2 * offset + width + start, STEP)].astype(jnp.float32)
                gate = gate.reshape(rows, STEP)
                up = up.reshape(rows, STEP)
                sigmoid = jax.nn.sigmoid(gate)
                active = gate * sigmoid
                low = (2 * index + half) * rows
                hidden[low : low + rows, pl.ds(start, STEP)] = (active * up).astype(jnp.bfloat16)
                place = pl.ds(offset + start, STEP)
                rates[0, half * rows : (half + 1) * rows, place] = up * (
                    sigmoid * (1.0 + gate * (1.0 - sigmoid))
                )
                rates[1, half * rows : (half + 1) * rows, place] = active

        offset += width

    for index in range(6):
        own, other = split_sides(tokens[:, index], side[0])
        target = turned if index < 3 else turned_out
        low = (index % 3) * 2 * rows
        target[:, low : low + 2 * rows] = jnp.concatenate([own, other], axis=0).T.astype(jnp.bfloat16)

    banded(widths, turned_out, hidden, totals, 0)

    @pl.loop(0, count // TILE)
    def _(block):
        here = pl.ds(pl.multiple_of(block * TILE, TILE), TILE)
        moved = jnp.dot(totals[...], chosen[:, here], preferred_element_type=jnp.float32)
        down_grad[here, :] = moved.T.astype(jnp.bfloat16)


def slopes_kernel(
    widths,
    chosen_far,
    own_up,
    other_up,
    rates_far,
    turned,
    gate_grad,
    up_grad,
    chosen,
    rates,
    gates,
    ups,
    totals,
    rate_sems,
    chosen_sems,
):
    count = chosen.shape[0]
    features = turned.shape[0]
    rows = own_up.shape[0]
    blocks = count // TILE
    starts = (0, widths[0], widths[0] + widths[1])

    def rate_copy(index):
        place = pl.ds(starts[index], widths[index])
        return pltpu.make_async_copy(
            rates_far.at[:, :, place], rates.at[:, :, place], rate_sems.at[index]
        )

    def chosen_copy(block):
        here = pl.ds(block * TILE, TILE)
        return pltpu.make_async_copy(
            chosen_far.at[here, :], chosen.at[here, :], chosen_sems.at[block]
        )

    for index in range(3):
        rate_copy(index).start()
    for block in range(blocks):
        chosen_copy(block).start()

    for index, width in enumerate(widths):
        offset = starts[index]
        rate_copy(index).wait()

        @pl.loop(0, width // STEP)
        def _(block, index=index, offset=offset):
            start = pl.multiple_of(block * STEP, STEP)
            place = pl.ds(pl.multiple_of(offset + start, STEP), STEP)
            for half, above in enumerate((own_up, other_up)):
                upstream = above[:, place].astype(jnp.float32)
                source = slice(half * rows, (half + 1) * rows)
                low = (2 * index + half) * rows
                gates[low : low + rows, pl.ds(start, STEP)] = (
                    upstream * rates[0, source, place]
                ).astype(jnp.bfloat16)
                ups[low : low + rows, pl.ds(start, STEP)] = (
                    upstream * rates[1, source, place]
                ).astype(jnp.bfloat16)

    banded(widths, turned, gates, totals, 0)
    banded(widths, turned, ups, totals, features)
    for block in range(blocks):
        chosen_copy(block).wait()

    @pl.loop(0, blocks)
    def _(block):
        here = pl.ds(pl.multiple_of(block * TILE, TILE), TILE)
        moved = jnp.dot(totals[...], chosen[:, here], preferred_element_type=jnp.float32)
        gate_grad[:, here] = moved[:features].astype(jnp.bfloat16)
        up_grad[:, here] = moved[features:].astype(jnp.bfloat16)


def per_device(
    ranks, down_weight, inputs, grad_out, gate_small, up_small, gate_mid, up_mid, gate_full, up_full
):
    n_dp = lax.axis_size("dp")
    n_tensor = lax.axis_size("tensor")
    n_rows = n_dp // 4
    count, features = down_weight.shape
    widths = tuple(padded(item.shape[1]) for item in (gate_small, gate_mid, gate_full))
    total = sum(widths)
    side = (lax.axis_index("dp") % 2)[None]
    core_swap = [(item, item ^ 1) for item in range(n_dp)]
    x_swap = [(item, item ^ 2) for item in range(n_dp)]
    by_place = [[4 * row + place for row in range(n_rows)] for place in range(4)]
    by_half = [
        [4 * row + 2 * half + core for row in range(n_rows) for core in range(2)] for half in range(2)
    ]

    def over_rows(blocks):
        return lax.all_to_all(blocks, "dp", 0, 0, axis_index_groups=by_place, tiled=True)

    given = (gate_small, up_small, gate_mid, up_mid, gate_full, up_full, inputs, grad_out)
    copies, local = pl.pallas_call(
        start_kernel,
        out_shape=(
            shaped((n_tensor, 6) + inputs.shape[1:]),
            shaped((gate_small.shape[0], 2 * total)),
        ),
        in_specs=[ANY] * len(given),
        out_specs=(VMEM, VMEM),
        scratch_shapes=[pltpu.VMEM(item.shape, item.dtype) for item in given]
        + [pltpu.SemaphoreType.DMA((len(given),))],
        compiler_params=FULL,
    )(*given)
    tokens = lax.all_to_all(copies, "tensor", 0, 0, tiled=True)

    position = (ranks // n_tensor)[None, :]
    ranked, chosen = call(
        sort_kernel, (shaped(down_weight.shape), shaped((count, count))), position, down_weight
    )

    there = lax.ppermute(local, "dp", x_swap)
    first = (lax.axis_index("dp") // 2) % 2 == 0
    two = jnp.concatenate([jnp.where(first, local, there), jnp.where(first, there, local)], axis=0)
    gathered = lax.all_gather(two, "dp", axis=0, axis_index_groups=by_half, tiled=True)
    pairs = gathered.reshape(n_rows, 2, two.shape[0], two.shape[1])

    rows = tokens.shape[0] * tokens.shape[2] // 2
    partial = functools.partial(partial_kernel, widths)
    sent = call(partial, shaped((rows, total)), 1 - side, tokens, ranked, scalars=1)
    other = lax.ppermute(sent, "dp", core_swap)
    kept = call(partial, shaped((rows, total), jnp.float32), side, tokens, ranked, scalars=1)
    summed = (kept + other.astype(jnp.float32)).astype(jnp.bfloat16)

    pieces = over_rows(summed.reshape(n_rows, -1, total))
    mine = jnp.sum(pieces.astype(jnp.float32), axis=0)
    theirs = lax.ppermute(mine.astype(jnp.bfloat16), "dp", x_swap)
    reduced = (mine + theirs.astype(jnp.float32)).astype(jnp.bfloat16)
    own_up = over_rows(jnp.broadcast_to(reduced[None], (n_rows,) + reduced.shape)).reshape(rows, total)

    down_grad, rates, turned = call(
        functools.partial(hidden_kernel, widths),
        (
            shaped((count, features)),
            shaped((2, 2 * rows, total), jnp.float32),
            shaped((features, 6 * rows)),
        ),
        side,
        chosen,
        pairs,
        tokens,
        scalars=1,
        scratch=(
            pltpu.VMEM((6 * rows, count), jnp.bfloat16),
            pltpu.VMEM((features, count), jnp.bfloat16),
            pltpu.VMEM((features, 6 * rows), jnp.bfloat16),
        ),
        flops=2 * features * count * (count + rows),
    )
    own_up = after(own_up, turned)
    other_up = lax.ppermute(own_up, "dp", core_swap)
    gate_grad, up_grad = pl.pallas_call(
        functools.partial(slopes_kernel, widths),
        out_shape=(shaped((features, count)),) * 2,
        in_specs=[ANY, VMEM, VMEM, ANY, VMEM],
        out_specs=(VMEM,) * 2,
        scratch_shapes=[
            pltpu.VMEM((count, count), jnp.bfloat16),
            pltpu.VMEM((2, 2 * rows, total), jnp.float32),
            pltpu.VMEM((6 * rows, count), jnp.bfloat16),
            pltpu.VMEM((6 * rows, count), jnp.bfloat16),
            pltpu.VMEM((2 * features, count), jnp.bfloat16),
            pltpu.SemaphoreType.DMA((3,)),
            pltpu.SemaphoreType.DMA((count // TILE,)),
        ],
        compiler_params=FULL,
        cost_estimate=pl.CostEstimate(
            flops=4 * features * count * (count + rows), bytes_accessed=2**24, transcendentals=0
        ),
    )(chosen, own_up, other_up, rates, turned)
    return (down_grad, gate_grad, up_grad)


def solution(mesh):
    return jax.shard_map(
        per_device,
        mesh=mesh,
        in_specs=(
            P("tensor"),
            P("tensor", "dp"),
            P(None, "tensor", "dp"),
            P(None, "tensor", "dp"),
            P("dp", "tensor"),
            P("dp", "tensor"),
            P("dp", "tensor"),
            P("dp", "tensor"),
            P("dp", "tensor"),
            P("dp", "tensor"),
        ),
        out_specs=(P("tensor", "dp"), P("dp", "tensor"), P("dp", "tensor")),
        check_vma=False,
    )
```

```python
import functools

import jax
import jax.numpy as jnp
from jax import lax
from jax.experimental import pallas as pl
from jax.experimental.pallas import tpu as pltpu
from jax.sharding import PartitionSpec as P

VMEM = pl.BlockSpec(memory_space=pltpu.VMEM)
ANY = pl.BlockSpec(memory_space=pl.ANY)
SMEM = pl.BlockSpec(memory_space=pltpu.SMEM)
LIMIT = pltpu.CompilerParams(vmem_limit_bytes=20 * 1024 * 1024)
FULL = pltpu.CompilerParams(vmem_limit_bytes=60 * 1024 * 1024)
TILE = 256
WEIGHT = 60
STEP = 128


def padded(width):
    return -(-width // 128) * 128


def call(kernel, out_shape, *args, scratch=(), scalars=0, flops=0):
    many = isinstance(out_shape, tuple)
    return pl.pallas_call(
        kernel,
        out_shape=out_shape,
        in_specs=[SMEM] * scalars + [VMEM] * (len(args) - scalars),
        out_specs=(VMEM,) * len(out_shape) if many else VMEM,
        scratch_shapes=list(scratch),
        compiler_params=LIMIT,
        cost_estimate=pl.CostEstimate(flops=flops, bytes_accessed=2**20, transcendentals=0),
    )(*args)


def shaped(shape, dtype=jnp.bfloat16):
    return jax.ShapeDtypeStruct(shape, dtype)


def after(value, other):
    def nothing(value_ref, other_ref, out_ref):
        pass

    return pl.pallas_call(
        nothing,
        out_shape=shaped(value.shape, value.dtype),
        in_specs=[VMEM, VMEM],
        out_specs=VMEM,
        input_output_aliases={0: 0},
        compiler_params=LIMIT,
    )(value, other)


def start_kernel(*refs):
    far, copies, packed = refs[:8], refs[8], refs[9]
    near, sems = refs[10:18], refs[18]
    moves = [
        pltpu.make_async_copy(source, target, sems.at[index])
        for index, (source, target) in enumerate(zip(far, near))
    ]
    for move in moves:
        move.start()
    for move in moves[:6]:
        move.wait()
    offset = 0
    for array in near[:6]:
        width = array.shape[1]
        wide = padded(width)
        if wide != width:
            packed[:, offset : offset + wide] = jnp.zeros((packed.shape[0], wide), packed.dtype)
        packed[:, offset : offset + width] = array[...]
        offset += wide
    for move in moves[6:]:
        move.wait()
    count = near[6].shape[0]

    @pl.loop(0, copies.shape[0])
    def _(place):
        copies[place, :count] = near[6][...]
        copies[place, count:] = near[7][...]


def sort_kernel(position, down, ranked, chosen):
    count = down.shape[0]

    @pl.loop(0, count // TILE)
    def _(block):
        here = pl.ds(pl.multiple_of(block * TILE, TILE), TILE)
        rows = lax.broadcasted_iota(jnp.int32, (TILE, count), 0) + block * TILE
        ones = (rows == position[...]).astype(jnp.float32).astype(jnp.bfloat16)
        chosen[here, :] = ones
        ranked[here, :] = jnp.dot(ones, down[...], preferred_element_type=jnp.float32).astype(
            jnp.bfloat16
        )


def pick(pair, place):
    return jnp.where(place == 0, pair[0], pair[1])


def group_of(block, core, half):
    places, rows, features = block.shape
    apart = block.astype(jnp.float32).reshape(places // 2, 2, 2, rows // 2, features)
    mine = pick((apart[:, 0], apart[:, 1]), half)
    return pick((mine[:, 0], mine[:, 1]), core).reshape(places * rows // 4, features)


def partial_kernel(widths, where, tokens, ranked, *rest):
    out = rest[-1]
    offset = 0
    for index, width in enumerate(widths):
        left = group_of(tokens[:, 3 + index], where[0], where[1])
        out[:, offset : offset + width] = lax.dot_general(
            left.astype(jnp.bfloat16),
            ranked[:width],
            (((1,), (1,)), ((), ())),
            preferred_element_type=jnp.float32,
        ).astype(out.dtype)
        offset += width


def banded(widths, across, stacked):
    bounds = (0,) + widths
    tokens = across.shape[1] // 3
    for band in range(3):
        low, high = bounds[band], bounds[band + 1]
        yield slice(low, high), jnp.dot(
            across[:, band * tokens :],
            stacked[band * tokens :, low:high],
            preferred_element_type=jnp.float32,
        )


def hidden_kernel(
    widths, where, chosen, pairs, tokens, down_grad, rates, turned, flag, hidden, totals, turned_out
):
    flag[...] = jnp.zeros_like(flag)
    count = chosen.shape[0]
    features = tokens.shape[3]
    rows = pairs.shape[0] * 8
    offset = 0
    for index, width in enumerate(widths):

        @pl.loop(0, width // STEP)
        def _(block, index=index, offset=offset, width=width):
            start = pl.multiple_of(block * STEP, STEP)
            for core in range(2):
                which = jnp.where(core == 0, where[0], 1 - where[0])
                gates = pairs[:, which, :, pl.ds(2 * offset + start, STEP)].astype(jnp.float32)
                ups = pairs[:, which, :, pl.ds(2 * offset + width + start, STEP)].astype(jnp.float32)
                gates = gates.reshape(-1, 2, 8, STEP)
                ups = ups.reshape(-1, 2, 8, STEP)
                for half in range(2):
                    gate = gates[:, half].reshape(rows, STEP)
                    up = ups[:, half].reshape(rows, STEP)
                    sigmoid = jax.nn.sigmoid(gate)
                    active = gate * sigmoid
                    group = (2 * half + core) * rows
                    low = 4 * index * rows + group
                    hidden[low : low + rows, pl.ds(start, STEP)] = (active * up).astype(jnp.bfloat16)
                    place = pl.ds(pl.multiple_of(offset + start, STEP), STEP)
                    rates[0, group : group + rows, place] = up * (
                        sigmoid * (1.0 + gate * (1.0 - sigmoid))
                    )
                    rates[1, group : group + rows, place] = active

        offset += width

    for index in range(6):
        block = tokens[:, index]
        for half in range(2):
            pair = [
                group_of(block, jnp.where(core == 0, where[0], 1 - where[0]), (where[1] + half) % 2)
                for core in range(2)
            ]
            flipped = jnp.concatenate(pair, axis=0).T.astype(jnp.bfloat16)
            if index < 3:
                turned[half, :, 2 * index * rows : 2 * (index + 1) * rows] = flipped
            else:
                low = (4 * (index - 3) + 2 * half) * rows
                turned_out[:, low : low + 2 * rows] = flipped

    for columns, product in banded(widths, turned_out, hidden):
        totals[:, columns] = product.astype(jnp.bfloat16)

    @pl.loop(0, count // TILE)
    def _(block):
        here = pl.ds(pl.multiple_of(block * TILE, TILE), TILE)
        moved = jnp.dot(totals[...], chosen[:, here], preferred_element_type=jnp.float32)
        down_grad[here, :] = moved.T.astype(jnp.bfloat16)


def slopes_of(widths, half, first, second, rates, gates, ups):
    rows = first.shape[0]
    offset = 0
    for index, width in enumerate(widths):

        @pl.loop(0, width // STEP)
        def _(block, index=index, offset=offset):
            start = pl.multiple_of(block * STEP, STEP)
            place = pl.ds(pl.multiple_of(offset + start, STEP), STEP)
            for core, above in enumerate((first, second)):
                upstream = above[:, place].astype(jnp.float32)
                source = slice((2 * half + core) * rows, (2 * half + core + 1) * rows)
                low = (2 * index + core) * rows
                gates[low : low + rows, pl.ds(start, STEP)] = (
                    upstream * rates[0, source, place]
                ).astype(jnp.bfloat16)
                ups[low : low + rows, pl.ds(start, STEP)] = (
                    upstream * rates[1, source, place]
                ).astype(jnp.bfloat16)

        offset += width


def first_kernel(widths, first, second, rates, turned, sums, gates, ups):
    features = turned.shape[1]
    slopes_of(widths, 0, first, second, rates, gates, ups)
    for place, array in enumerate((gates, ups)):
        for columns, product in banded(widths, turned[0], array):
            sums[place * features : (place + 1) * features, columns] = product


def second_kernel(
    widths, chosen, first, second, rates, turned, sums, gate_grad, up_grad, gates, ups, totals
):
    count = chosen.shape[0]
    features = turned.shape[1]
    slopes_of(widths, 1, first, second, rates, gates, ups)
    for place, array in enumerate((gates, ups)):
        for columns, product in banded(widths, turned[1], array):
            low = slice(place * features, (place + 1) * features)
            totals[low, columns] = (sums[low, columns] + product).astype(jnp.bfloat16)

    @pl.loop(0, count // TILE)
    def _(block):
        here = pl.ds(pl.multiple_of(block * TILE, TILE), TILE)
        moved = jnp.dot(totals[...], chosen[:, here], preferred_element_type=jnp.float32)
        gate_grad[:, here] = moved[:features].astype(jnp.bfloat16)
        up_grad[:, here] = moved[features:].astype(jnp.bfloat16)


def per_device(
    ranks, down_weight, inputs, grad_out, gate_small, up_small, gate_mid, up_mid, gate_full, up_full
):
    n_dp = lax.axis_size("dp")
    n_tensor = lax.axis_size("tensor")
    n_rows = n_dp // 4
    count, features = down_weight.shape
    widths = tuple(padded(item.shape[1]) for item in (gate_small, gate_mid, gate_full))
    total = sum(widths)
    place = lax.axis_index("dp")
    core, half = place % 2, (place // 2) % 2
    core_swap = [(item, item ^ 1) for item in range(n_dp)]
    x_swap = [(item, item ^ 2) for item in range(n_dp)]
    by_place = [[4 * row + place for row in range(n_rows)] for place in range(4)]
    by_half = [
        [4 * row + 2 * half + core for row in range(n_rows) for core in range(2)] for half in range(2)
    ]

    def over_rows(blocks):
        return lax.all_to_all(blocks, "dp", 0, 0, axis_index_groups=by_place, tiled=True)

    given = (gate_small, up_small, gate_mid, up_mid, gate_full, up_full, inputs, grad_out)
    copies, local = pl.pallas_call(
        start_kernel,
        out_shape=(
            shaped((n_tensor, 6) + inputs.shape[1:]),
            shaped((gate_small.shape[0], 2 * total)),
        ),
        in_specs=[ANY] * len(given),
        out_specs=(VMEM, VMEM),
        scratch_shapes=[pltpu.VMEM(item.shape, item.dtype) for item in given]
        + [pltpu.SemaphoreType.DMA((len(given),))],
        compiler_params=FULL,
    )(*given)
    tokens = lax.all_to_all(copies, "tensor", 0, 0, tiled=True)

    position = (ranks // n_tensor)[None, :]
    ranked, chosen = call(
        sort_kernel,
        (shaped(down_weight.shape), shaped((count, count))),
        position,
        down_weight,
        flops=2 * count * count * features,
    )

    there = lax.ppermute(local, "dp", x_swap)
    two = jnp.concatenate([local, there], axis=0)
    gathered = lax.all_gather(two, "dp", axis=0, axis_index_groups=by_half, tiled=True)
    pairs = gathered.reshape(n_rows, 2, two.shape[0], two.shape[1])

    rows = tokens.shape[0] * tokens.shape[2] // 4

    def partial(core, half, dtype, *behind):
        return call(
            functools.partial(partial_kernel, widths),
            shaped((rows, total), dtype),
            jnp.stack([core, half]),
            tokens,
            ranked,
            *behind,
            scalars=1,
            flops=2 * WEIGHT * rows * total * features,
        )

    def core_sum(half, *behind):
        sent = partial(1 - core, half, jnp.bfloat16, *behind)
        other = lax.ppermute(sent, "dp", core_swap)
        return partial(core, half, jnp.float32) + other.astype(jnp.float32), sent

    across, behind = core_sum(1 - half)
    far = lax.ppermute(across.astype(jnp.bfloat16), "dp", x_swap)
    summed = (core_sum(half, behind)[0] + far.astype(jnp.float32)).astype(jnp.bfloat16)
    pieces = over_rows(summed.reshape(n_rows, -1, total))
    reduced = jnp.sum(pieces.astype(jnp.float32), axis=0).astype(jnp.bfloat16)
    near = over_rows(jnp.broadcast_to(reduced[None], (n_rows,) + reduced.shape)).reshape(rows, total)

    down_grad, rates, turned, flag = call(
        functools.partial(hidden_kernel, widths),
        (
            shaped((count, features)),
            shaped((2, 4 * rows, total), jnp.float32),
            shaped((2, features, 6 * rows)),
            shaped((8, 128), jnp.float32),
        ),
        jnp.stack([core, half]),
        chosen,
        pairs,
        tokens,
        scalars=1,
        scratch=(
            pltpu.VMEM((12 * rows, count), jnp.bfloat16),
            pltpu.VMEM((features, count), jnp.bfloat16),
            pltpu.VMEM((features, 12 * rows), jnp.bfloat16),
        ),
        flops=2 * features * count * (count + rows),
    )
    near = after(near, flag)
    beyond = lax.ppermute(near, "dp", x_swap)
    near_other = lax.ppermute(near, "dp", core_swap)
    halves = (pltpu.VMEM((6 * rows, count), jnp.bfloat16),) * 2
    sums = call(
        functools.partial(first_kernel, widths),
        shaped((2 * features, count), jnp.float32),
        near,
        near_other,
        rates,
        turned,
        scratch=halves,
        flops=4 * features * count * rows,
    )
    beyond = after(beyond, sums)
    beyond_other = lax.ppermute(beyond, "dp", core_swap)
    gate_grad, up_grad = call(
        functools.partial(second_kernel, widths),
        (shaped((features, count)),) * 2,
        chosen,
        beyond,
        beyond_other,
        rates,
        turned,
        sums,
        scratch=halves + (pltpu.VMEM((2 * features, count), jnp.bfloat16),),
        flops=4 * features * count * (count + rows),
    )
    return (down_grad, gate_grad, up_grad)


def solution(mesh):
    return jax.shard_map(
        per_device,
        mesh=mesh,
        in_specs=(
            P("tensor"),
            P("tensor", "dp"),
            P(None, "tensor", "dp"),
            P(None, "tensor", "dp"),
            P("dp", "tensor"),
            P("dp", "tensor"),
            P("dp", "tensor"),
            P("dp", "tensor"),
            P("dp", "tensor"),
            P("dp", "tensor"),
        ),
        out_specs=(P("tensor", "dp"), P("dp", "tensor"), P("dp", "tensor")),
        check_vma=False,
    )
```

```python
import functools

import jax
import jax.numpy as jnp
from jax import lax
from jax.experimental import pallas as pl
from jax.experimental.pallas import tpu as pltpu
from jax.sharding import PartitionSpec as P

VMEM = pl.BlockSpec(memory_space=pltpu.VMEM)
ANY = pl.BlockSpec(memory_space=pl.ANY)
SMEM = pl.BlockSpec(memory_space=pltpu.SMEM)
LIMIT = pltpu.CompilerParams(vmem_limit_bytes=20 * 1024 * 1024)
FULL = pltpu.CompilerParams(vmem_limit_bytes=60 * 1024 * 1024)
TILE = 256
WEIGHT = 110
STEP = 128


def padded(width):
    return -(-width // 128) * 128


def call(kernel, out_shape, *args, scratch=(), scalars=0, flops=0):
    many = isinstance(out_shape, tuple)
    return pl.pallas_call(
        kernel,
        out_shape=out_shape,
        in_specs=[SMEM] * scalars + [VMEM] * (len(args) - scalars),
        out_specs=(VMEM,) * len(out_shape) if many else VMEM,
        scratch_shapes=list(scratch),
        compiler_params=LIMIT,
        cost_estimate=pl.CostEstimate(flops=flops, bytes_accessed=2**20, transcendentals=0),
    )(*args)


def shaped(shape, dtype=jnp.bfloat16):
    return jax.ShapeDtypeStruct(shape, dtype)


def after(value, other):
    def nothing(value_ref, other_ref, out_ref):
        pass

    return pl.pallas_call(
        nothing,
        out_shape=shaped(value.shape, value.dtype),
        in_specs=[VMEM, VMEM],
        out_specs=VMEM,
        input_output_aliases={0: 0},
        compiler_params=LIMIT,
    )(value, other)


def start_kernel(*refs):
    far, copies, packed = refs[:8], refs[8], refs[9]
    near, sems = refs[10:18], refs[18]
    moves = [
        pltpu.make_async_copy(source, target, sems.at[index])
        for index, (source, target) in enumerate(zip(far, near))
    ]
    for move in moves:
        move.start()
    for move in moves[:6]:
        move.wait()
    offset = 0
    for array in near[:6]:
        width = array.shape[1]
        wide = padded(width)
        if wide != width:
            packed[:, offset : offset + wide] = jnp.zeros((packed.shape[0], wide), packed.dtype)
        packed[:, offset : offset + width] = array[...]
        offset += wide
    for move in moves[6:]:
        move.wait()
    count = near[6].shape[0]

    @pl.loop(0, copies.shape[0])
    def _(place):
        copies[place, :count] = near[6][...]
        copies[place, count:] = near[7][...]


def sort_kernel(position, down, down_far, ranked, chosen, flag):
    flag[...] = jnp.zeros_like(flag)
    count, features = down.shape

    @pl.loop(0, count // TILE)
    def _(block):
        here = pl.ds(pl.multiple_of(block * TILE, TILE), TILE)
        rows = lax.broadcasted_iota(jnp.int32, (TILE, count), 0) + block * TILE
        ones = (rows == position[...]).astype(jnp.float32).astype(jnp.bfloat16)
        chosen[here, :] = ones
        for low, source in ((0, down), (features, down_far)):
            ranked[here, low : low + features] = jnp.dot(
                ones, source[...], preferred_element_type=jnp.float32
            ).astype(jnp.bfloat16)


def pick(pair, place):
    return jnp.where(place == 0, pair[0], pair[1])


def group_of(block, core, half):
    places, rows, features = block.shape
    apart = block.astype(jnp.float32).reshape(places // 2, 2, 2, rows // 2, features)
    mine = pick((apart[:, 0], apart[:, 1]), half)
    return pick((mine[:, 0], mine[:, 1]), core).reshape(places * rows // 4, features)


def split_kernel(where, tokens, flag, sent, kept):
    rows = sent.shape[1] // 2
    for index in range(3):
        block = tokens[:, 3 + index]
        for half in range(2):
            for out, core in ((sent, 1 - where[0]), (kept, where[0])):
                out[index, half * rows : (half + 1) * rows, :] = group_of(
                    block, core, (where[1] + half) % 2
                ).astype(jnp.bfloat16)


def partial_kernel(widths, half, kept, other, ranked, *rest):
    out = rest[-1]
    rows = out.shape[0]
    offset = 0
    for index, width in enumerate(widths):
        here = slice(half * rows, (half + 1) * rows)
        left = jnp.concatenate([kept[index, here, :], other[index, here, :]], axis=1)
        out[:, offset : offset + width] = lax.dot_general(
            left, ranked[:width], (((1,), (1,)), ((), ())), preferred_element_type=jnp.float32
        ).astype(out.dtype)
        offset += width


def banded(widths, across, stacked):
    bounds = (0,) + widths
    tokens = across.shape[1] // 3
    for band in range(3):
        low, high = bounds[band], bounds[band + 1]
        yield slice(low, high), jnp.dot(
            across[:, band * tokens :],
            stacked[band * tokens :, low:high],
            preferred_element_type=jnp.float32,
        )


def rates_kernel(widths, where, pairs, hidden, rates, flag):
    flag[...] = jnp.zeros_like(flag)
    rows = pairs.shape[0] * 8
    offset = 0
    for index, width in enumerate(widths):

        @pl.loop(0, width // STEP)
        def _(block, index=index, offset=offset, width=width):
            start = pl.multiple_of(block * STEP, STEP)
            for core in range(2):
                which = jnp.where(core == 0, where[0], 1 - where[0])
                gates = pairs[:, which, :, pl.ds(2 * offset + start, STEP)].astype(jnp.float32)
                ups = pairs[:, which, :, pl.ds(2 * offset + width + start, STEP)].astype(jnp.float32)
                gates = gates.reshape(-1, 2, 8, STEP)
                ups = ups.reshape(-1, 2, 8, STEP)
                for half in range(2):
                    gate = gates[:, half].reshape(rows, STEP)
                    up = ups[:, half].reshape(rows, STEP)
                    sigmoid = jax.nn.sigmoid(gate)
                    active = gate * sigmoid
                    group = (2 * half + core) * rows
                    low = 4 * index * rows + group
                    hidden[low : low + rows, pl.ds(start, STEP)] = (active * up).astype(jnp.bfloat16)
                    place = pl.ds(pl.multiple_of(offset + start, STEP), STEP)
                    rates[0, group : group + rows, place] = up * (
                        sigmoid * (1.0 + gate * (1.0 - sigmoid))
                    )
                    rates[1, group : group + rows, place] = active

        offset += width


def down_kernel(widths, where, chosen, hidden, tokens, down_grad, turned, flag, totals, turned_out):
    flag[...] = jnp.zeros_like(flag)
    count = chosen.shape[0]
    rows = turned.shape[2] // 6
    for index in range(6):
        block = tokens[:, index]
        for half in range(2):
            pair = [
                group_of(block, jnp.where(core == 0, where[0], 1 - where[0]), (where[1] + half) % 2)
                for core in range(2)
            ]
            flipped = jnp.concatenate(pair, axis=0).T.astype(jnp.bfloat16)
            if index < 3:
                turned[half, :, 2 * index * rows : 2 * (index + 1) * rows] = flipped
            else:
                low = (4 * (index - 3) + 2 * half) * rows
                turned_out[:, low : low + 2 * rows] = flipped

    for columns, product in banded(widths, turned_out, hidden):
        totals[:, columns] = product.astype(jnp.bfloat16)

    @pl.loop(0, count // TILE)
    def _(block):
        here = pl.ds(pl.multiple_of(block * TILE, TILE), TILE)
        moved = jnp.dot(totals[...], chosen[:, here], preferred_element_type=jnp.float32)
        down_grad[here, :] = moved.T.astype(jnp.bfloat16)


def slopes_of(widths, half, first, second, rates, gates, ups):
    rows = first.shape[0]
    offset = 0
    for index, width in enumerate(widths):

        @pl.loop(0, width // STEP)
        def _(block, index=index, offset=offset):
            start = pl.multiple_of(block * STEP, STEP)
            place = pl.ds(pl.multiple_of(offset + start, STEP), STEP)
            for core, above in enumerate((first, second)):
                upstream = above[:, place].astype(jnp.float32)
                source = slice((2 * half + core) * rows, (2 * half + core + 1) * rows)
                low = (2 * index + core) * rows
                gates[low : low + rows, pl.ds(start, STEP)] = (
                    upstream * rates[0, source, place]
                ).astype(jnp.bfloat16)
                ups[low : low + rows, pl.ds(start, STEP)] = (
                    upstream * rates[1, source, place]
                ).astype(jnp.bfloat16)

        offset += width


def first_kernel(widths, first, second, rates, turned, sums, gates, ups):
    features = turned.shape[1]
    slopes_of(widths, 0, first, second, rates, gates, ups)
    for place, array in enumerate((gates, ups)):
        for columns, product in banded(widths, turned[0], array):
            sums[place * features : (place + 1) * features, columns] = product


def second_kernel(
    widths, chosen, first, second, rates, turned, sums, gate_grad, up_grad, gates, ups, totals
):
    count = chosen.shape[0]
    features = turned.shape[1]
    slopes_of(widths, 1, first, second, rates, gates, ups)
    for place, array in enumerate((gates, ups)):
        for columns, product in banded(widths, turned[1], array):
            low = slice(place * features, (place + 1) * features)
            totals[low, columns] = (sums[low, columns] + product).astype(jnp.bfloat16)

    @pl.loop(0, count // TILE)
    def _(block):
        here = pl.ds(pl.multiple_of(block * TILE, TILE), TILE)
        moved = jnp.dot(totals[...], chosen[:, here], preferred_element_type=jnp.float32)
        gate_grad[:, here] = moved[:features].astype(jnp.bfloat16)
        up_grad[:, here] = moved[features:].astype(jnp.bfloat16)


def per_device(
    ranks, down_weight, inputs, grad_out, gate_small, up_small, gate_mid, up_mid, gate_full, up_full
):
    n_dp = lax.axis_size("dp")
    n_tensor = lax.axis_size("tensor")
    n_rows = n_dp // 4
    count, features = down_weight.shape
    widths = tuple(padded(item.shape[1]) for item in (gate_small, gate_mid, gate_full))
    total = sum(widths)
    place = lax.axis_index("dp")
    core, half = place % 2, (place // 2) % 2
    core_swap = [(item, item ^ 1) for item in range(n_dp)]
    x_swap = [(item, item ^ 2) for item in range(n_dp)]
    by_place = [[4 * row + place for row in range(n_rows)] for place in range(4)]
    by_half = [
        [4 * row + 2 * half + core for row in range(n_rows) for core in range(2)] for half in range(2)
    ]

    def over_rows(blocks):
        return lax.all_to_all(blocks, "dp", 0, 0, axis_index_groups=by_place, tiled=True)

    given = (gate_small, up_small, gate_mid, up_mid, gate_full, up_full, inputs, grad_out)
    copies, local = pl.pallas_call(
        start_kernel,
        out_shape=(
            shaped((n_tensor, 6) + inputs.shape[1:]),
            shaped((gate_small.shape[0], 2 * total)),
        ),
        in_specs=[ANY] * len(given),
        out_specs=(VMEM, VMEM),
        scratch_shapes=[pltpu.VMEM(item.shape, item.dtype) for item in given]
        + [pltpu.SemaphoreType.DMA((len(given),))],
        compiler_params=FULL,
    )(*given)
    tokens = lax.all_to_all(copies, "tensor", 0, 0, tiled=True)

    position = (ranks // n_tensor)[None, :]
    down_far = lax.ppermute(down_weight, "dp", core_swap)
    flag_shape = shaped((8, 128), jnp.float32)
    ranked, chosen, flag = call(
        sort_kernel,
        (shaped((count, 2 * features)), shaped((count, count)), flag_shape),
        position,
        down_weight,
        down_far,
        flops=4 * count * count * features,
    )

    there = lax.ppermute(local, "dp", x_swap)
    two = jnp.concatenate([local, there], axis=0)
    gathered = lax.all_gather(two, "dp", axis=0, axis_index_groups=by_half, tiled=True)
    pairs = gathered.reshape(n_rows, 2, two.shape[0], two.shape[1])

    rows = tokens.shape[0] * tokens.shape[2] // 4

    where = jnp.stack([core, half])
    sent, kept = call(
        split_kernel, (shaped((3, 2 * rows, features)),) * 2, where, tokens, flag, scalars=1
    )
    other = lax.ppermute(sent, "dp", core_swap)

    def partial(half, dtype, *behind):
        return call(
            functools.partial(partial_kernel, widths, half),
            shaped((rows, total), dtype),
            kept,
            other,
            ranked,
            *behind,
            flops=4 * WEIGHT * rows * total * features,
        )

    across = partial(1, jnp.bfloat16)
    far = lax.ppermute(across, "dp", x_swap)
    summed = (partial(0, jnp.float32, across) + far.astype(jnp.float32)).astype(jnp.bfloat16)
    pieces = over_rows(summed.reshape(n_rows, -1, total))
    hidden, rates, flag = call(
        functools.partial(rates_kernel, widths),
        (shaped((12 * rows, count)), shaped((2, 4 * rows, total), jnp.float32), flag_shape),
        where,
        pairs,
        scalars=1,
        flops=2 * features * count * count,
    )
    pieces = after(pieces, flag)
    reduced = jnp.sum(pieces.astype(jnp.float32), axis=0).astype(jnp.bfloat16)
    near = over_rows(jnp.broadcast_to(reduced[None], (n_rows,) + reduced.shape)).reshape(rows, total)

    down_grad, turned, flag = call(
        functools.partial(down_kernel, widths),
        (shaped((count, features)), shaped((2, features, 6 * rows)), flag_shape),
        where,
        chosen,
        hidden,
        tokens,
        scalars=1,
        scratch=(
            pltpu.VMEM((features, count), jnp.bfloat16),
            pltpu.VMEM((features, 12 * rows), jnp.bfloat16),
        ),
        flops=2 * features * count * (count + rows),
    )
    near = after(near, flag)
    beyond = lax.ppermute(near, "dp", x_swap)
    near_other = lax.ppermute(near, "dp", core_swap)
    halves = (pltpu.VMEM((6 * rows, count), jnp.bfloat16),) * 2
    sums = call(
        functools.partial(first_kernel, widths),
        shaped((2 * features, count), jnp.float32),
        near,
        near_other,
        rates,
        turned,
        scratch=halves,
        flops=4 * features * count * rows,
    )
    beyond = after(beyond, sums)
    beyond_other = lax.ppermute(beyond, "dp", core_swap)
    gate_grad, up_grad = call(
        functools.partial(second_kernel, widths),
        (shaped((features, count)),) * 2,
        chosen,
        beyond,
        beyond_other,
        rates,
        turned,
        sums,
        scratch=halves + (pltpu.VMEM((2 * features, count), jnp.bfloat16),),
        flops=4 * features * count * (count + rows),
    )
    return (down_grad, gate_grad, up_grad)


def solution(mesh):
    return jax.shard_map(
        per_device,
        mesh=mesh,
        in_specs=(
            P("tensor"),
            P("tensor", "dp"),
            P(None, "tensor", "dp"),
            P(None, "tensor", "dp"),
            P("dp", "tensor"),
            P("dp", "tensor"),
            P("dp", "tensor"),
            P("dp", "tensor"),
            P("dp", "tensor"),
            P("dp", "tensor"),
        ),
        out_specs=(P("tensor", "dp"), P("dp", "tensor"), P("dp", "tensor")),
        check_vma=False,
    )
```

```python
import functools

import jax
import jax.numpy as jnp
from jax import lax
from jax.experimental import pallas as pl
from jax.experimental.pallas import tpu as pltpu
from jax.sharding import PartitionSpec as P

VMEM = pl.BlockSpec(memory_space=pltpu.VMEM)
ANY = pl.BlockSpec(memory_space=pl.ANY)
SMEM = pl.BlockSpec(memory_space=pltpu.SMEM)
LIMIT = pltpu.CompilerParams(vmem_limit_bytes=20 * 1024 * 1024)
FULL = pltpu.CompilerParams(vmem_limit_bytes=60 * 1024 * 1024)
TILE = 256
WEIGHT = 85
REDUCE = 58
STEP = 128


def padded(width):
    return -(-width // 128) * 128


def call(kernel, out_shape, *args, scratch=(), scalars=0, flops=0):
    many = isinstance(out_shape, tuple)
    return pl.pallas_call(
        kernel,
        out_shape=out_shape,
        in_specs=[SMEM] * scalars + [VMEM] * (len(args) - scalars),
        out_specs=(VMEM,) * len(out_shape) if many else VMEM,
        scratch_shapes=list(scratch),
        compiler_params=LIMIT,
        cost_estimate=pl.CostEstimate(flops=flops, bytes_accessed=2**20, transcendentals=0),
    )(*args)


def shaped(shape, dtype=jnp.bfloat16):
    return jax.ShapeDtypeStruct(shape, dtype)


def after(value, other):
    def nothing(value_ref, other_ref, out_ref):
        pass

    return pl.pallas_call(
        nothing,
        out_shape=shaped(value.shape, value.dtype),
        in_specs=[VMEM, ANY],
        out_specs=VMEM,
        input_output_aliases={0: 0},
        compiler_params=LIMIT,
    )(value, other)


def start_kernel(*refs):
    far, copies, packed = refs[:8], refs[8], refs[9]
    near, sems = refs[10:18], refs[18]
    moves = [
        pltpu.make_async_copy(source, target, sems.at[index])
        for index, (source, target) in enumerate(zip(far, near))
    ]
    for move in moves:
        move.start()
    for move in moves[:6]:
        move.wait()
    offset = 0
    for array in near[:6]:
        width = array.shape[1]
        wide = padded(width)
        if wide != width:
            packed[:, offset : offset + wide] = jnp.zeros((packed.shape[0], wide), packed.dtype)
        packed[:, offset : offset + width] = array[...]
        offset += wide
    for move in moves[6:]:
        move.wait()
    count = near[6].shape[0]

    @pl.loop(0, copies.shape[0])
    def _(place):
        copies[place, :count] = near[6][...]
        copies[place, count:] = near[7][...]


def ones_where(rows, columns):
    return (rows == columns).astype(jnp.float32).astype(jnp.bfloat16)


def sort_kernel(position, down, ranked, flag):
    flag[...] = jnp.zeros_like(flag)
    count = down.shape[0]

    @pl.loop(0, count // TILE)
    def _(block):
        here = pl.ds(pl.multiple_of(block * TILE, TILE), TILE)
        rows = lax.broadcasted_iota(jnp.int32, (TILE, count), 0) + block * TILE
        ranked[here, :] = jnp.dot(
            ones_where(rows, position[...]), down[...], preferred_element_type=jnp.float32
        ).astype(jnp.bfloat16)


def own_place():
    place = lax.axis_index("dp")
    return place % 2, (place // 2) % 2


def pick(pair, place):
    return jnp.where(place == 0, pair[0], pair[1])


def group_of(block, core, half):
    places, rows, features = block.shape
    apart = block.astype(jnp.float32).reshape(places // 2, 2, 2, rows // 2, features)
    mine = pick((apart[:, 0], apart[:, 1]), half)
    return pick((mine[:, 0], mine[:, 1]), core).reshape(places * rows // 4, features)


def split_kernel(tokens, flag, sent, kept):
    own_core, own_half = own_place()
    rows = sent.shape[1] // 2
    for index in range(3):
        block = tokens[:, 3 + index]
        for half in range(2):
            for out, core in ((sent, 1 - own_core), (kept, own_core)):
                out[index, half * rows : (half + 1) * rows, :] = group_of(
                    block, core, (own_half + half) % 2
                ).astype(jnp.bfloat16)


def partial_kernel(widths, half, kept, other, ranked, ranked_far, *rest):
    out = rest[-1]
    rows = out.shape[0]
    offset = 0
    for index, width in enumerate(widths):
        here = slice(half * rows, (half + 1) * rows)
        total = None
        for left, right in ((kept, ranked), (other, ranked_far)):
            term = lax.dot_general(
                left[index, here, :],
                right[:width],
                (((1,), (1,)), ((), ())),
                preferred_element_type=jnp.float32,
            )
            total = term if total is None else total + term
        out[:, offset : offset + width] = total.astype(out.dtype)
        offset += width


def banded(widths, across, stacked):
    bounds = (0,) + widths
    tokens = across.shape[1] // 3
    for band in range(3):
        low, high = bounds[band], bounds[band + 1]
        yield slice(low, high), jnp.dot(
            across[:, band * tokens :],
            stacked[band * tokens :, low:high],
            preferred_element_type=jnp.float32,
        )


def rates_kernel(
    widths, parts, pairs, hidden, rates, near, hidden_near, rates_near, in_sems, out_sems
):
    own_core, _ = own_place()
    rows = pairs.shape[0] * 8
    starts = (0, widths[0], widths[0] + widths[1])

    def loads(number):
        index, low, size = parts[number]
        for which in range(2):
            place = pl.ds(2 * starts[index] + which * widths[index] + low, size)
            yield pltpu.make_async_copy(
                pairs.at[:, :, :, place], near.at[:, :, :, place], in_sems.at[number, which]
            )

    def stores(number):
        index, low, size = parts[number]
        place = pl.ds(starts[index] + low, size)
        yield pltpu.make_async_copy(
            rates_near.at[:, :, place], rates.at[:, :, place], out_sems.at[number, 0]
        )
        spot = (pl.ds(4 * index * rows, 4 * rows), pl.ds(low, size))
        yield pltpu.make_async_copy(hidden_near.at[spot], hidden.at[spot], out_sems.at[number, 1])

    for number in range(len(parts)):
        for copy in loads(number):
            copy.start()
    for number, (index, low, size) in enumerate(parts):
        for copy in loads(number):
            copy.wait()
        offset, width = starts[index], widths[index]

        @pl.loop(0, size // STEP)
        def _(block, index=index, low=low, offset=offset, width=width):
            start = pl.multiple_of(low + block * STEP, STEP)
            gate_place = pl.ds(pl.multiple_of(2 * offset + start, STEP), STEP)
            up_place = pl.ds(pl.multiple_of(2 * offset + width + start, STEP), STEP)
            for core in range(2):
                which = jnp.where(core == 0, own_core, 1 - own_core)
                gates = near[:, which, :, gate_place].astype(jnp.float32).reshape(-1, 2, 8, STEP)
                ups = near[:, which, :, up_place].astype(jnp.float32).reshape(-1, 2, 8, STEP)
                for half in range(2):
                    gate = gates[:, half].reshape(rows, STEP)
                    up = ups[:, half].reshape(rows, STEP)
                    sigmoid = jax.nn.sigmoid(gate)
                    active = gate * sigmoid
                    group = (2 * half + core) * rows
                    row = 4 * index * rows + group
                    hidden_near[row : row + rows, pl.ds(start, STEP)] = (active * up).astype(
                        jnp.bfloat16
                    )
                    place = pl.ds(pl.multiple_of(offset + start, STEP), STEP)
                    rates_near[0, group : group + rows, place] = up * (
                        sigmoid * (1.0 + gate * (1.0 - sigmoid))
                    )
                    rates_near[1, group : group + rows, place] = active

        for copy in stores(number):
            copy.start()
    for number in range(len(parts)):
        for copy in stores(number):
            copy.wait()


def reduce_kernel(pieces, rates, out):
    total = pieces[0].astype(jnp.float32)
    for place in range(1, pieces.shape[0]):
        total = total + pieces[place].astype(jnp.float32)
    total = total.astype(jnp.bfloat16)
    for place in range(out.shape[0]):
        out[place] = total


def turn(tokens, index, half):
    own_core, own_half = own_place()
    pair = [
        group_of(tokens[:, index], jnp.where(core == 0, own_core, 1 - own_core), (own_half + half) % 2)
        for core in range(2)
    ]
    return jnp.concatenate(pair, axis=0).T.astype(jnp.bfloat16)


def down_kernel(widths, position, hidden_far, tokens, down_grad, flag, hidden, totals, turned, sems):
    flag[...] = jnp.zeros_like(flag)
    count = position.shape[1]
    rows = hidden.shape[0] // 12

    def load(index):
        spot = (pl.ds(4 * index * rows, 4 * rows), pl.ds(0, widths[index]))
        return pltpu.make_async_copy(hidden_far.at[spot], hidden.at[spot], sems.at[index])

    for index in range(3):
        load(index).start()
    for index in range(3):
        for half in range(2):
            low = (4 * index + 2 * half) * rows
            turned[:, low : low + 2 * rows] = turn(tokens, 3 + index, half)
    for index in range(3):
        load(index).wait()
    for columns, product in banded(widths, turned, hidden):
        totals[:, columns] = product.astype(jnp.bfloat16)

    @pl.loop(0, count // TILE)
    def _(block):
        here = pl.ds(pl.multiple_of(block * TILE, TILE), TILE)
        ranks_here = lax.broadcasted_iota(jnp.int32, (count, TILE), 0)
        moved = jnp.dot(
            totals[...],
            ones_where(ranks_here, position[:, here]),
            preferred_element_type=jnp.float32,
        )
        down_grad[here, :] = moved.T.astype(jnp.bfloat16)


def slopes_of(widths, first, second, rates, gates, ups):
    rows = first.shape[0]
    offset = 0
    for index, width in enumerate(widths):

        @pl.loop(0, width // STEP)
        def _(block, index=index, offset=offset):
            start = pl.multiple_of(block * STEP, STEP)
            place = pl.ds(pl.multiple_of(offset + start, STEP), STEP)
            for core, above in enumerate((first, second)):
                upstream = above[:, place].astype(jnp.float32)
                source = slice(core * rows, (core + 1) * rows)
                low = (2 * index + core) * rows
                gates[low : low + rows, pl.ds(start, STEP)] = (
                    upstream * rates[0, source, place]
                ).astype(jnp.bfloat16)
                ups[low : low + rows, pl.ds(start, STEP)] = (
                    upstream * rates[1, source, place]
                ).astype(jnp.bfloat16)

        offset += width


def first_kernel(
    widths,
    position,
    first,
    second,
    rates_far,
    tokens,
    sums,
    chosen,
    rates_second,
    turned_second,
    rates,
    turned,
    gates,
    ups,
    sems,
):
    count = position.shape[1]
    features = tokens.shape[3]
    rows = first.shape[0]
    copies = [
        pltpu.make_async_copy(
            rates_far.at[:, pl.ds(2 * half * rows, 2 * rows), :], target, sems.at[half]
        )
        for half, target in enumerate((rates, rates_second))
    ]
    for copy in copies:
        copy.start()
    for index in range(3):
        here = slice(2 * index * rows, 2 * (index + 1) * rows)
        turned[:, here] = turn(tokens, index, 0)
        turned_second[:, here] = turn(tokens, index, 1)

    @pl.loop(0, count // TILE)
    def _(block):
        here = pl.ds(pl.multiple_of(block * TILE, TILE), TILE)
        chosen[here, :] = ones_where(
            lax.broadcasted_iota(jnp.int32, (TILE, count), 0) + block * TILE, position[...]
        )

    copies[0].wait()
    slopes_of(widths, first, second, rates, gates, ups)
    for place, array in enumerate((gates, ups)):
        for columns, product in banded(widths, turned, array):
            sums[place * features : (place + 1) * features, columns] = product
    copies[1].wait()


def second_kernel(
    widths,
    chosen,
    first,
    second,
    rates,
    turned,
    sums,
    gate_grad,
    up_grad,
    gates,
    ups,
    totals,
    staged,
    sems,
):
    count = chosen.shape[0]
    features = turned.shape[0]
    slopes_of(widths, first, second, rates, gates, ups)
    for place, array in enumerate((gates, ups)):
        for columns, product in banded(widths, turned, array):
            low = slice(place * features, (place + 1) * features)
            totals[low, columns] = (sums[low, columns] + product).astype(jnp.bfloat16)

    def stores(block):
        here = pl.ds(block * TILE, TILE)
        for place, target in enumerate((gate_grad, up_grad)):
            yield pltpu.make_async_copy(
                staged.at[pl.ds(place * features, features), here],
                target.at[:, here],
                sems.at[block, place],
            )

    for block in range(count // TILE):
        here = slice(block * TILE, (block + 1) * TILE)
        staged[:, here] = jnp.dot(
            totals[...], chosen[:, here], preferred_element_type=jnp.float32
        ).astype(jnp.bfloat16)
        for copy in stores(block):
            copy.start()
    for block in range(count // TILE):
        for copy in stores(block):
            copy.wait()


def per_device(
    ranks, down_weight, inputs, grad_out, gate_small, up_small, gate_mid, up_mid, gate_full, up_full
):
    n_dp = lax.axis_size("dp")
    n_tensor = lax.axis_size("tensor")
    n_rows = n_dp // 4
    count, features = down_weight.shape
    widths = tuple(padded(item.shape[1]) for item in (gate_small, gate_mid, gate_full))
    total = sum(widths)
    core_swap = [(item, item ^ 1) for item in range(n_dp)]
    x_swap = [(item, item ^ 2) for item in range(n_dp)]
    by_place = [[4 * row + place for row in range(n_rows)] for place in range(4)]
    by_half = [
        [4 * row + 2 * half + core for row in range(n_rows) for core in range(2)] for half in range(2)
    ]

    def over_rows(blocks):
        return lax.all_to_all(blocks, "dp", 0, 0, axis_index_groups=by_place, tiled=True)

    given = (gate_small, up_small, gate_mid, up_mid, gate_full, up_full, inputs, grad_out)
    copies, local = pl.pallas_call(
        start_kernel,
        out_shape=(
            shaped((n_tensor, 6) + inputs.shape[1:]),
            shaped((gate_small.shape[0], 2 * total)),
        ),
        in_specs=[ANY] * len(given),
        out_specs=(VMEM, VMEM),
        scratch_shapes=[pltpu.VMEM(item.shape, item.dtype) for item in given]
        + [pltpu.SemaphoreType.DMA((len(given),))],
        compiler_params=FULL,
    )(*given)
    tokens = lax.all_to_all(copies, "tensor", 0, 0, tiled=True)

    position = (ranks // n_tensor)[None, :]
    flag_shape = shaped((8, 128), jnp.float32)
    ranked, flag = call(
        sort_kernel,
        (shaped((count, features)), flag_shape),
        position,
        down_weight,
        flops=2 * count * count * features,
    )
    ranked_far = lax.ppermute(ranked, "dp", core_swap)

    there = lax.ppermute(local, "dp", x_swap)
    two = jnp.concatenate([local, there], axis=0)
    gathered = lax.all_gather(two, "dp", axis=0, axis_index_groups=by_half, tiled=True)
    pairs = gathered.reshape(n_rows, 2, two.shape[0], two.shape[1])

    rows = tokens.shape[0] * tokens.shape[2] // 4

    sent, kept = call(split_kernel, (shaped((3, 2 * rows, features)),) * 2, tokens, flag)
    other = lax.ppermute(sent, "dp", core_swap)

    def partial(half, dtype, *behind):
        return call(
            functools.partial(partial_kernel, widths, half),
            shaped((rows, total), dtype),
            kept,
            other,
            ranked,
            ranked_far,
            *behind,
            flops=4 * WEIGHT * rows * total * features,
        )

    across = partial(1, jnp.bfloat16)
    far = lax.ppermute(across, "dp", x_swap)
    summed = (partial(0, jnp.float32, across) + far.astype(jnp.float32)).astype(jnp.bfloat16)
    pieces = over_rows(summed.reshape(n_rows, -1, total))
    half_full = widths[2] // 2
    parts = ((2, 0, half_full), (2, half_full, half_full), (1, 0, widths[1]), (0, 0, widths[0]))
    hidden_shape, rates_shape = (12 * rows, count), (2, 4 * rows, total)
    hidden, rates = pl.pallas_call(
        functools.partial(rates_kernel, widths, parts),
        out_shape=(shaped(hidden_shape), shaped(rates_shape, jnp.float32)),
        in_specs=[ANY],
        out_specs=(ANY, ANY),
        scratch_shapes=[
            pltpu.VMEM(pairs.shape, jnp.bfloat16),
            pltpu.VMEM(hidden_shape, jnp.bfloat16),
            pltpu.VMEM(rates_shape, jnp.float32),
            pltpu.SemaphoreType.DMA((len(parts), 2)),
            pltpu.SemaphoreType.DMA((len(parts), 2)),
        ],
        compiler_params=FULL,
        cost_estimate=pl.CostEstimate(
            flops=2 * features * count * count, bytes_accessed=2**20, transcendentals=0
        ),
    )(pairs)
    reduced = pl.pallas_call(
        reduce_kernel,
        out_shape=shaped(pieces.shape),
        in_specs=[VMEM, ANY],
        out_specs=VMEM,
        compiler_params=pltpu.CompilerParams(vmem_limit_bytes=REDUCE * 1024 * 1024),
    )(pieces, rates)
    near = over_rows(reduced).reshape(rows, total)

    down_grad, flag = pl.pallas_call(
        functools.partial(down_kernel, widths),
        out_shape=(shaped((count, features)), flag_shape),
        in_specs=[VMEM, ANY, VMEM],
        out_specs=(VMEM, VMEM),
        scratch_shapes=[
            pltpu.VMEM(hidden_shape, jnp.bfloat16),
            pltpu.VMEM((features, count), jnp.bfloat16),
            pltpu.VMEM((features, 12 * rows), jnp.bfloat16),
            pltpu.SemaphoreType.DMA((3,)),
        ],
        compiler_params=LIMIT,
        cost_estimate=pl.CostEstimate(
            flops=2 * features * count * count, bytes_accessed=2**20, transcendentals=0
        ),
    )(position, hidden, tokens)
    near = after(near, flag)
    beyond = lax.ppermute(near, "dp", x_swap)
    near_other = lax.ppermute(near, "dp", core_swap)
    halves = [pltpu.VMEM((6 * rows, count), jnp.bfloat16)] * 2
    rates_half, turned_shape = (2, 2 * rows, total), (features, 6 * rows)
    sums, chosen, rates_second, turned = pl.pallas_call(
        functools.partial(first_kernel, widths),
        out_shape=(
            shaped((2 * features, count), jnp.float32),
            shaped((count, count)),
            shaped(rates_half, jnp.float32),
            shaped(turned_shape),
        ),
        in_specs=[VMEM, VMEM, VMEM, ANY, VMEM],
        out_specs=(VMEM,) * 4,
        scratch_shapes=[
            pltpu.VMEM(rates_half, jnp.float32),
            pltpu.VMEM(turned_shape, jnp.bfloat16),
            *halves,
            pltpu.SemaphoreType.DMA((2,)),
        ],
        compiler_params=pltpu.CompilerParams(vmem_limit_bytes=37 * 1024 * 1024),
        cost_estimate=pl.CostEstimate(
            flops=4 * features * count * rows, bytes_accessed=2**20, transcendentals=0
        ),
    )(position, near, near_other, rates, tokens)
    beyond = after(beyond, sums)
    beyond_other = lax.ppermute(beyond, "dp", core_swap)
    gate_grad, up_grad = pl.pallas_call(
        functools.partial(second_kernel, widths),
        out_shape=(shaped((features, count)),) * 2,
        in_specs=[VMEM] * 6,
        out_specs=(ANY, ANY),
        scratch_shapes=[
            *halves,
            pltpu.VMEM((2 * features, count), jnp.bfloat16),
            pltpu.VMEM((2 * features, count), jnp.bfloat16),
            pltpu.SemaphoreType.DMA((count // TILE, 2)),
        ],
        compiler_params=LIMIT,
        cost_estimate=pl.CostEstimate(
            flops=4 * features * count * (count + rows), bytes_accessed=2**20, transcendentals=0
        ),
    )(chosen, beyond, beyond_other, rates_second, turned, sums)
    return (down_grad, gate_grad, up_grad)


def solution(mesh):
    return jax.shard_map(
        per_device,
        mesh=mesh,
        in_specs=(
            P("tensor"),
            P("tensor", "dp"),
            P(None, "tensor", "dp"),
            P(None, "tensor", "dp"),
            P("dp", "tensor"),
            P("dp", "tensor"),
            P("dp", "tensor"),
            P("dp", "tensor"),
            P("dp", "tensor"),
            P("dp", "tensor"),
        ),
        out_specs=(P("tensor", "dp"), P("dp", "tensor"), P("dp", "tensor")),
        check_vma=False,
    )
```
